128 devices in a mesh: seq: 8 (over y_lo, x), dp: 16 (over z, y_hi, core).
Axes of the slice: x: 4, y: 4 (y_hi: 2, y_lo: 2; y = y_hi * 2 + y_lo), z: 4, core: 2. Of those that a mesh axis runs over, the one named last changes fastest.
Arguments:
- inputs: float32 [16, 2048, 768], P('dp', 'seq'), may hold values from -6 to 6
- routes: int32 [16, 2048, 2], P('dp', 'seq'), may hold values from 0 to 15, all different within a row; in each aligned block of 256 rows (0 to 255, 256 to 511, ..., all dimensions but the last counted through in order) at most 40 rows name the same one
- buckets: int32 [2048], replicated, may hold values from 0 to 31, as said below
- norm1_gain: bfloat16 [768], P(('seq', 'dp')), may hold values from 0.5 to 1.5
- qkv_weight: bfloat16 [768, 2304], P(('seq', 'dp')), may hold values from -0.3125 to 0.3125
- out_weight: bfloat16 [768, 768], P(('seq', 'dp')), may hold values from -0.875 to 0.875
- rel_bias: bfloat16 [384], P(('seq', 'dp')), may hold values from -3 to 3
- norm2_gain: bfloat16 [768], P(('seq', 'dp')), may hold values from 0.5 to 1.5
- router_projection_weight: bfloat16 [768, 16], P(('seq', 'dp')), may hold values from -0.15625 to 0.15625
- expert_in: bfloat16 [16, 768, 3072], P('dp', None, 'seq'), may hold values from -0.21875 to 0.21875
- expert_out: bfloat16 [16, 3072, 768], P('dp', 'seq'), may hold values from -0.15625 to 0.15625
- cotangent: float32 [16, 2048, 768], P('dp', 'seq'), may hold values from -6 to 6
Outputs:
- layer_out: float32 [16, 2048, 768], P('dp', 'seq')
- input_grad: float32 [16, 2048, 768], P('dp', 'seq')
- norm1_grad: float32 [768], P(('seq', 'dp'))
- qkv_grad: float32 [768, 2304], P(('seq', 'dp'))
- out_grad: float32 [768, 768], P(('seq', 'dp'))
- bias_grad: float32 [384], P(('seq', 'dp'))
- norm2_grad: float32 [768], P(('seq', 'dp'))
- router_grad: float32 [768, 16], P(('seq', 'dp'))
- expert_in_grad: float32 [16, 768, 3072], P('dp', None, 'seq')
- expert_out_grad: float32 [16, 3072, 768], P('dp', 'seq')
The draws below stay inside these ranges and needn't reach their ends.
Inputs may be any that keep to these rules, and one draw needn't show every extreme that they name: `routes`: in the rows of one sequence on one device (aligned blocks of 256 token rows) no expert is named more than 40 times, a bound that some block reaches; a token's two experts differ. `buckets`: the bucket never falls as the distance grows; each distance below 16 has a bucket of its own, and the largest distance has bucket 32 - 1.
All inputs are finite; a program needn't handle non-finite values.
Results may differ from the reference program's by a relative error of at most 0.025.
Values may be sent and summed in bfloat16 or wider, within the bound.
No kernel may reach another device: no remote copies, remote signals or barrier semaphores. Data moves between devices by JAX's collectives and lax.ppermute only.
A program may use at most 256 MiB of HBM per device.

```python
import math
import jax
import jax.numpy as jnp
import numpy as np
from jax import lax

D = 768
HEADS = 12
HEAD_DIM = 64
FF = 3072
BUCKETS = 32
SEQ_LEN = 2048
NSEQ = 16
EXPERTS = 16
CAP = 40
N_SEQ = 8


def draw_buckets(key, part):
    key = jax.random.fold_in(key, 11)
    distance = jnp.arange(SEQ_LEN, dtype=jnp.int32)
    spread_range = SEQ_LEN - BUCKETS // 2
    rises = (jax.random.randint(key, (SEQ_LEN,), 0, spread_range) < BUCKETS // 2).astype(jnp.int32)
    rises = jnp.where(distance < BUCKETS // 2, 1, rises)
    rises = jnp.where(distance == 0, 0, rises)
    levels = jnp.minimum(jnp.cumsum(rises), BUCKETS - 1)
    return jnp.where(distance == SEQ_LEN - 1, BUCKETS - 1, levels).astype(jnp.int32)


def block_scale(own_key, extent, shards, low, high):
    loudness, own = 1.0, jax.random.fold_in(own_key, 6)
    for position, parts in shards:
        draws = jnp.exp(jax.random.uniform(jax.random.fold_in(own, position), (parts,), jnp.float32, low / len(shards), high / len(shards)))
        loudness = loudness * jnp.repeat(draws, extent[position] // parts).reshape([-1 if axis == position else 1 for axis in range(len(extent))])
    return loudness


def deal_out(rng, own, number, rows, number_of, top, most, skew):
    order = jax.random.permutation(rng, number_of)
    packed, usual = shares(number_of, rows * top, most, skew, True), shares(number_of, rows * top, most, skew, False)
    places = jnp.arange(number_of)

    def named(lengths, turn):
        used = int((lengths > 0).sum())
        fixed = max(1, used // 4)
        shifted = fixed + (places - fixed + turn * (used - fixed)) % max(1, number_of - fixed)
        return jnp.zeros((number_of,), jnp.int32).at[order[jnp.where(places < fixed, places, shifted)]].set(jnp.asarray(lengths, jnp.int32))

    lengths = jnp.where(number % 4 == 0, named(packed, number // 4), named(usual, number - number // 4 - 1))
    mixed = jax.random.permutation(jax.random.fold_in(own, 3), number_of)
    source_of, taker = mixed[0:number_of // 2 * 2:2], mixed[1:number_of // 2 * 2:2]
    slack = jnp.minimum(lengths[source_of] - 1, most - lengths[taker]) // 2
    slack = jnp.where((source_of == order[0]) | (taker == order[0]) | (lengths[taker] == 0), 0, jnp.maximum(slack, 0))
    shifted = jax.random.randint(jax.random.fold_in(own, 4), (number_of // 2,), 0, 1 << 20) % (slack + 1)
    lengths = lengths.at[source_of].add(-shifted).at[taker].add(shifted)
    members = jnp.searchsorted(jnp.cumsum(lengths), jnp.arange(rows * top), side="right").astype(jnp.int32)
    grid = members.reshape(top, rows).T
    grid = grid[jax.random.permutation(jax.random.fold_in(own, 1), rows)]
    turn = jax.random.randint(jax.random.fold_in(own, 2), (rows, 1), 0, top)
    return jnp.take_along_axis(grid, (jnp.arange(top)[None, :] + turn) % top, axis=1)


def shares(amount, total, reach, skew, full):
    portions = [(1 << 20) // math.isqrt(grade ** skew) + 1 for grade in range(1, amount + 1)]
    largest = reach if full else min(reach, max(-(-total // amount), total * portions[0] // sum(portions)))
    least = 1 if total - largest >= amount - 1 else 0
    counts, surplus = [largest] + [least] * (amount - 1), total - largest - least * (amount - 1)
    while surplus > 0:
        candidates = [i for i in range(1, amount) if counts[i] < largest] or [i for i in range(1, amount) if counts[i] < reach]
        mass, left = sum([portions[i] for i in candidates]), surplus
        for i in candidates:
            extra = min(reach - counts[i], max(1, left * portions[i] // mass), surplus)
            counts[i] = counts[i] + extra
            surplus = surplus - extra
    return np.array(counts)


def scatter_about(key, extent, scale, limit, shards=(), kind=jnp.bfloat16):
    drawn = scale * jax.random.normal(key, extent, jnp.float32)
    if shards:
        drawn = drawn * block_scale(key, extent, shards, -0.22, 0.18)
    return jnp.clip(drawn, -limit, limit).astype(kind)


def setup_inputs(seed: int = 0) -> dict:
    keys = jax.random.split(jax.random.key(seed), 13)
    inputs = scatter_about(keys[0], (NSEQ, SEQ_LEN, D), 1.0, 6.0, ((0, 16), (1, 8)), jnp.float32)
    routes_keys = jax.random.split(jax.random.fold_in(keys[1], 1), NSEQ * SEQ_LEN // (SEQ_LEN // N_SEQ))
    routes_turns = jax.random.permutation(jax.random.fold_in(keys[1], 3), NSEQ * SEQ_LEN // (SEQ_LEN // N_SEQ))
    routes = jax.vmap(lambda own, number: deal_out(jax.random.fold_in(keys[1], 2), own, number, SEQ_LEN // N_SEQ, EXPERTS, 2, CAP, 2))(routes_keys, routes_turns).reshape((NSEQ, SEQ_LEN, 2))
    buckets = draw_buckets(jax.random.fold_in(keys[12], 71), 0)
    norm1_gain = jnp.clip(1.0 + 0.1 * jax.random.normal(keys[3], (D,), jnp.float32), 0.5, 1.5).astype(jnp.bfloat16)
    qkv_weight = scatter_about(keys[4], (D, 3 * D), (D // 2) ** -0.5, 0.3125, ((0, 128),))
    out_weight = scatter_about(keys[5], (D, D), (D // 16) ** -0.5, 0.875, ((0, 128),))
    rel_bias = scatter_about(keys[6], (HEADS * BUCKETS,), 0.5, 3.0, ((0, 128),))
    norm2_gain = jnp.clip(1.0 + 0.1 * jax.random.normal(keys[7], (D,), jnp.float32), 0.5, 1.5).astype(jnp.bfloat16)
    router_projection_weight = scatter_about(keys[8], (D, EXPERTS), (2 * D) ** -0.5, 0.15625, ((0, 128),))
    expert_in = scatter_about(keys[9], (EXPERTS, D, FF), D ** -0.5, 0.21875, ((0, 16), (2, 8)))
    expert_out = scatter_about(keys[10], (EXPERTS, FF, D), (FF // 2) ** -0.5, 0.15625, ((0, 16), (1, 8)))
    cotangent = scatter_about(keys[11], (NSEQ, SEQ_LEN, D), 1.0, 6.0, ((0, 16), (1, 8)), jnp.float32)
    return dict(inputs=inputs, routes=routes, buckets=buckets, norm1_gain=norm1_gain, qkv_weight=qkv_weight, out_weight=out_weight, rel_bias=rel_bias, norm2_gain=norm2_gain, router_projection_weight=router_projection_weight, expert_in=expert_in, expert_out=expert_out, cotangent=cotangent)


@jax.custom_vjp
def low(v):
    return lax.optimization_barrier(v.astype(jnp.bfloat16)).astype(jnp.float32)

@jax.custom_vjp
def low_back(v):
    return v

def low_keep(v):
    return (low(v), None)

def low_pass(kept, grad):
    return (grad,)

def back_keep(v):
    return (v, None)

def back_low(kept, grad):
    return (low(grad),)
low.defvjp(low_keep, low_pass)
low_back.defvjp(back_keep, back_low)
highest = lax.Precision.HIGHEST

def rms_scale(value, gain):
    return value * lax.rsqrt(lax.optimization_barrier(jnp.mean(value * value, axis=-1, keepdims=True)) + 1e-06) * gain

def attend(seq_rows, qkv_weight, out_weight, relative_bias_lookup, buckets):
    length = seq_rows.shape[0]
    qkv = low(low_back(jnp.dot(seq_rows, qkv_weight, precision=highest)))
    queries = qkv[:, :D].reshape(length, HEADS, HEAD_DIM)
    key_rows = qkv[:, D:2 * D].reshape(length, HEADS, HEAD_DIM)
    value_rows = qkv[:, 2 * D:].reshape(length, HEADS, HEAD_DIM)
    places = jnp.arange(length, dtype=jnp.int32)
    distance = (places[:, None] - places[None, :]).astype(jnp.int32)
    causal = distance >= 0
    bucket_onehot_matrix = (buckets[:, None] == jnp.arange(BUCKETS, dtype=jnp.int32)[None, :]).astype(relative_bias_lookup.dtype)
    dist_table = jnp.dot(relative_bias_lookup, bucket_onehot_matrix.T, precision=highest)
    position_bias = jnp.take(dist_table, jnp.clip(distance, 0, length - 1).astype(jnp.int32), axis=1)
    score_scale = 1.0 / math.sqrt(HEAD_DIM)
    raw_scores = jnp.einsum('qhd,khd->hqk', queries, key_rows, precision=highest) * score_scale + position_bias
    scores = jnp.where(causal[None], low_back(raw_scores), -1e+30)
    probs = jax.nn.softmax(scores, axis=-1)
    attended = jnp.einsum('hqk,khd->qhd', low(probs), value_rows, precision=highest).reshape(length, D)
    attended = low(low_back(attended))
    return low_back(jnp.dot(attended, out_weight, precision=highest))

def layer(inputs, gain_one, qkv_weight, out_weight, rel_bias, gain_two, router_projection_weight, expert_in, expert_out, positions, routes, buckets):
    h_one = low(rms_scale(inputs, gain_one))
    relative_bias_lookup = rel_bias.reshape(HEADS, BUCKETS)
    branch = lax.map(jax.checkpoint(lambda seq_rows: attend(seq_rows, qkv_weight, out_weight, relative_bias_lookup, buckets)), h_one)
    middle = inputs + branch
    h_two = low(rms_scale(middle, gain_two))
    token_count = h_two.shape[0] * h_two.shape[1]
    flat_rows = h_two.reshape(token_count, D)
    route_pairs = routes.reshape(token_count, 2).astype(jnp.int32)
    logits = jnp.dot(flat_rows, router_projection_weight, precision=highest)
    chosen = jnp.take_along_axis(logits, route_pairs, axis=1)
    gate_values = jax.nn.softmax(chosen, axis=1)
    padded = jnp.concatenate([flat_rows, jnp.zeros((1, D), flat_rows.dtype)], axis=0)

    def one_expert(expert_items):
        expert_places, weight_in, weight_out = expert_items
        token_rows = low_back(padded[(expert_places // 2).astype(jnp.int32)])
        preact = low_back(jnp.dot(token_rows, weight_in, precision=highest))
        activated = low(jax.nn.gelu(preact, approximate=False))
        return low(low_back(jnp.dot(activated, weight_out, precision=highest)))
    results = lax.map(jax.checkpoint(one_expert), (positions, expert_in, expert_out))
    combined = jnp.zeros((2 * token_count + 1, D), results.dtype).at[positions.reshape(-1)].add(results.reshape(-1, D))
    combined = combined[:2 * token_count].reshape(token_count, 2, D)
    mixture = lax.optimization_barrier(jnp.sum(gate_values[:, :, None] * combined, axis=1))
    return middle + mixture.reshape(inputs.shape)

def reference(inputs, routes, buckets, norm1_gain, qkv_weight, out_weight, rel_bias, norm2_gain, router_projection_weight, expert_in, expert_out, cotangent):
    token_count = NSEQ * SEQ_LEN
    assigned = routes.reshape(token_count * 2).astype(jnp.int32)
    sorted_order = jnp.argsort(assigned, stable=True).astype(jnp.int32)
    expert_range = jnp.arange(EXPERTS, dtype=jnp.int32)
    expert_counts = lax.optimization_barrier(jnp.sum((assigned[:, None] == expert_range[None, :]).astype(jnp.int32), axis=0))
    expert_starts = (jnp.cumsum(expert_counts) - expert_counts).astype(jnp.int32)
    row_limit = NSEQ * N_SEQ * CAP
    offsets = jnp.arange(row_limit, dtype=jnp.int32)
    lookup = jnp.minimum(expert_starts[:, None] + offsets[None, :], token_count * 2 - 1).astype(jnp.int32)
    positions = jnp.where(offsets[None, :] < expert_counts[:, None], sorted_order[lookup], token_count * 2).astype(jnp.int32)

    def forward(inputs_f, gain_one, qkv_f, out_f, bias_f, gain_two, router_f, in_f, out_e):
        return layer(inputs_f, gain_one, qkv_f, out_f, bias_f, gain_two, router_f, in_f, out_e, positions, routes, buckets)
    primals = (inputs.astype(jnp.float32), norm1_gain.astype(jnp.float32), qkv_weight.astype(jnp.float32), out_weight.astype(jnp.float32), rel_bias.astype(jnp.float32), norm2_gain.astype(jnp.float32), router_projection_weight.astype(jnp.float32), expert_in.astype(jnp.float32), expert_out.astype(jnp.float32))
    layer_out, pullback = jax.vjp(forward, *primals)
    grads = pullback(cotangent.astype(jnp.float32))
    return (layer_out, grads[0], grads[1], grads[2], grads[3], grads[4], grads[5], grads[6], grads[7], grads[8])
```

```python
import math

import jax
import jax.numpy as jnp
from jax import lax
from jax.experimental import pallas as pl
from jax.experimental.pallas import tpu as pltpu
from jax.sharding import Mesh
from jax.sharding import PartitionSpec as P

D = 768
HEADS = 12
HEAD_DIM = 64
BUCKETS = 32
DP = ("dp_0", "dp_1", "dp_2")
SEQ = ("seq_0", "seq_1")
SEQ_DP = SEQ + DP
N_SEQ = 8
N_DP = 16
N_ALL = N_SEQ * N_DP
SHARD = D // N_ALL
ROWS = 256
LENGTH = N_SEQ * ROWS
TILES = LENGTH // ROWS
CHUNK = 2 * ROWS
PAIR = 2 * HEAD_DIM
GROUP = 3 * PAIR
MASKED = -1e30
VMEM_LIMIT = 56 * 1024 * 1024
NT = (((1,), (1,)), ((), ()))
F32 = jnp.float32
BF16 = jnp.bfloat16


def exchange(value, axes):
    return lax.all_to_all(value, axes, split_axis=0, concat_axis=0, tiled=True)


def after(value, earlier):
    return lax.optimization_barrier((value, earlier))[0]


def normalize(values):
    multiplier = lax.rsqrt(jnp.mean(values * values, axis=-1, keepdims=True) + 1e-06)
    return (values * multiplier, multiplier)


def norm_back(grad_normed, normed, multiplier):
    return multiplier * (
        grad_normed - normed * jnp.mean(grad_normed * normed, axis=-1, keepdims=True)
    )


def two_parts(value):
    high = lax.reduce_precision(value, 8, 7)
    return high.astype(BF16), (value - high).astype(BF16)


def fill_tiles(bias_ref, tiles_ref):
    for h in range(2):
        for b in range(TILES):
            low = LENGTH - ROWS * b
            row = jnp.concatenate(
                [bias_ref[h : h + 1, low : low + ROWS], bias_ref[h : h + 1, low - ROWS : low]], axis=1
            )
            turned = pltpu.roll(
                jnp.broadcast_to(row, (ROWS, 2 * ROWS)), 0, 1, stride=1, stride_axis=0
            )
            tiles_ref[h, ROWS * b : ROWS * (b + 1), :] = turned[:, :ROWS]
        tiles_ref[h, LENGTH:, :] = jnp.full((ROWS, ROWS), MASKED, F32)


def work_item(items_ref, n):
    block = items_ref[n]
    head = (n >= TILES).astype(jnp.int32)
    start = pl.multiple_of(block * ROWS, ROWS)
    offset = (TILES - 1 - block) * ROWS
    chunks = (block + 2) // 2
    mine = lax.broadcasted_iota(jnp.int32, (ROWS, PAIR), 1) // HEAD_DIM == head
    return block, head, start, offset, chunks, mine


def forward_kernel(items_ref, bias_ref, qkv_ref, out_ref, lse_ref, tiles_ref, vt_ref, s_ref):
    fill_tiles(bias_ref, tiles_ref)
    vt_ref[...] = qkv_ref[:, 2 * PAIR :].T
    out_ref[...] = jnp.zeros_like(out_ref)

    def item(n, carry):
        block, head, start, offset, chunks, mine = work_item(items_ref, n)
        q = qkv_ref[pl.ds(start, ROWS), :PAIR]
        q = jnp.where(mine, q.astype(F32) * (1.0 / math.sqrt(HEAD_DIM)), 0.0).astype(BF16)

        def score(c, top):
            at = pl.multiple_of(c * CHUNK, CHUNK)
            k = qkv_ref[pl.ds(at, CHUNK), PAIR : 2 * PAIR]
            s = lax.dot_general(k, q, NT, preferred_element_type=F32)
            s = s + tiles_ref[head, pl.ds(pl.multiple_of(offset + at, ROWS), CHUNK), :]
            s_ref[pl.ds(at, CHUNK), :] = s
            return jnp.maximum(top, jnp.max(s, axis=0, keepdims=True))

        top = lax.fori_loop(0, chunks, score, jnp.full((1, ROWS), MASKED, F32))

        def mix(c, sums):
            total, acc = sums
            at = pl.multiple_of(c * CHUNK, CHUNK)
            p = jnp.exp(s_ref[pl.ds(at, CHUNK), :] - top)
            acc = acc + jnp.dot(
                vt_ref[:, pl.ds(at, CHUNK)], p.astype(BF16), preferred_element_type=F32
            )
            return total + jnp.sum(p, axis=0, keepdims=True), acc

        total, acc = lax.fori_loop(
            0, chunks, mix, (jnp.zeros((1, ROWS), F32), jnp.zeros((PAIR, ROWS), F32))
        )
        lse_ref[head, block] = top + jnp.log(total)
        old = out_ref[pl.ds(start, ROWS), :].astype(F32)
        out_ref[pl.ds(start, ROWS), :] = jnp.where(mine, (acc / total).T, old).astype(BF16)
        return carry

    lax.fori_loop(0, TILES + TILES // 2, item, 0)


def backward_kernel(
    items_ref, bias_ref, qkv_ref, grad_ref, lse_ref, dqkv_ref, dbias_ref,
    tiles_ref, kt_ref, p_ref, dp_ref, dtiles_ref, dk_ref, dv_ref,
):
    fill_tiles(bias_ref, tiles_ref)
    kt_ref[...] = qkv_ref[:, PAIR : 2 * PAIR].T
    dtiles_ref[...] = jnp.zeros_like(dtiles_ref)
    dk_ref[...] = jnp.zeros_like(dk_ref)
    dv_ref[...] = jnp.zeros_like(dv_ref)
    dqkv_ref[:, :PAIR] = jnp.zeros((LENGTH, PAIR), BF16)
    dbias_ref[...] = jnp.zeros_like(dbias_ref)
    scale = 1.0 / math.sqrt(HEAD_DIM)

    def item(n, carry):
        block, head, start, offset, chunks, mine = work_item(items_ref, n)
        q = qkv_ref[pl.ds(start, ROWS), :PAIR]
        q = jnp.where(mine, q.astype(F32) * scale, 0.0).astype(BF16)
        g = jnp.where(mine, grad_ref[pl.ds(start, ROWS), :].astype(F32), 0.0).astype(BF16)
        lse = lse_ref[head, block]

        def first(c, inner):
            at = pl.multiple_of(c * CHUNK, CHUNK)
            k = qkv_ref[pl.ds(at, CHUNK), PAIR : 2 * PAIR]
            v = qkv_ref[pl.ds(at, CHUNK), 2 * PAIR :]
            s = lax.dot_general(k, q, NT, preferred_element_type=F32)
            s = s + tiles_ref[head, pl.ds(pl.multiple_of(offset + at, ROWS), CHUNK), :]
            p = jnp.exp(s - lse)
            dp = lax.dot_general(v, g, NT, preferred_element_type=F32)
            p_ref[pl.ds(at, CHUNK), :] = p
            dp_ref[pl.ds(at, CHUNK), :] = dp
            return inner + jnp.sum(p * dp, axis=0, keepdims=True)

        inner = lax.fori_loop(0, chunks, first, jnp.zeros((1, ROWS), F32))

        def second(c, dq):
            at = pl.multiple_of(c * CHUNK, CHUNK)
            p = p_ref[pl.ds(at, CHUNK), :]
            ds = p * (dp_ref[pl.ds(at, CHUNK), :] - inner)
            there = pl.ds(pl.multiple_of(offset + at, ROWS), CHUNK)
            dtiles_ref[head, there, :] = dtiles_ref[head, there, :] + ds
            ds = ds.astype(BF16)
            here = pl.ds(at, CHUNK)
            dk_ref[here, :] = dk_ref[here, :] + jnp.dot(ds, q, preferred_element_type=F32)
            dv_ref[here, :] = dv_ref[here, :] + jnp.dot(
                p.astype(BF16), g, preferred_element_type=F32
            )
            return dq + jnp.dot(kt_ref[:, here], ds, preferred_element_type=F32)

        dq = lax.fori_loop(0, chunks, second, jnp.zeros((PAIR, ROWS), F32))
        old = dqkv_ref[pl.ds(start, ROWS), :PAIR].astype(F32)
        dqkv_ref[pl.ds(start, ROWS), :PAIR] = jnp.where(mine, (dq * scale).T, old).astype(BF16)
        return carry

    lax.fori_loop(0, TILES + TILES // 2, item, 0)
    dqkv_ref[:, PAIR : 2 * PAIR] = dk_ref[...].astype(BF16)
    dqkv_ref[:, 2 * PAIR :] = dv_ref[...].astype(BF16)
    row_of = lax.broadcasted_iota(jnp.int32, (8, 2 * ROWS), 0)
    for h in range(2):
        for b in range(TILES):
            part = dtiles_ref[h, ROWS * b : ROWS * (b + 1), :]
            part = jnp.concatenate([part, jnp.zeros_like(part)], axis=1)
            half = ROWS // 2
            while half >= 8:
                part = part[:half] + pltpu.roll(part[half:], 2 * ROWS - half, 1)
                half //= 2
            for bit in (4, 2, 1):
                part = jnp.where(
                    (row_of & bit) != 0, pltpu.roll(part, 2 * ROWS - bit, 1), part
                )
            line = jnp.sum(part, axis=0, keepdims=True)
            low = LENGTH - ROWS * b
            dbias_ref[h : h + 1, low : low + ROWS] += line[:, :ROWS]
            dbias_ref[h : h + 1, low - ROWS : low] += line[:, ROWS:]


def in_vmem(count):
    return [pl.BlockSpec(memory_space=pltpu.VMEM)] * count


def attention_forward(items, bias, qkv):
    return pl.pallas_call(
        forward_kernel,
        out_shape=(
            jax.ShapeDtypeStruct((LENGTH, PAIR), BF16),
            jax.ShapeDtypeStruct((2, TILES, 1, ROWS), F32),
        ),
        in_specs=[pl.BlockSpec(memory_space=pltpu.SMEM)] + in_vmem(2),
        out_specs=tuple(in_vmem(2)),
        scratch_shapes=[
            pltpu.VMEM((2, LENGTH + ROWS, ROWS), F32),
            pltpu.VMEM((PAIR, LENGTH), BF16),
            pltpu.VMEM((LENGTH, ROWS), F32),
        ],
        compiler_params=pltpu.CompilerParams(vmem_limit_bytes=VMEM_LIMIT),
        name="attention_forward",
    )(items, bias, qkv)


def attention_backward(items, bias, qkv, grad, lse):
    return pl.pallas_call(
        backward_kernel,
        out_shape=(
            jax.ShapeDtypeStruct((LENGTH, GROUP), BF16),
            jax.ShapeDtypeStruct((8, LENGTH + ROWS), F32),
        ),
        in_specs=[pl.BlockSpec(memory_space=pltpu.SMEM)] + in_vmem(4),
        out_specs=tuple(in_vmem(2)),
        scratch_shapes=[
            pltpu.VMEM((2, LENGTH + ROWS, ROWS), F32),
            pltpu.VMEM((PAIR, LENGTH), BF16),
            pltpu.VMEM((LENGTH, ROWS), F32),
            pltpu.VMEM((LENGTH, ROWS), F32),
            pltpu.VMEM((2, LENGTH + ROWS, ROWS), F32),
            pltpu.VMEM((LENGTH, PAIR), F32),
            pltpu.VMEM((LENGTH, PAIR), F32),
        ],
        compiler_params=pltpu.CompilerParams(vmem_limit_bytes=VMEM_LIMIT),
        name="attention_backward",
    )(items, bias, qkv, grad, lse)


ERFC = (
    0.22562630138780296, 0.22657565341666724, 0.2009589960079044, 0.19696137866341243, 0.07151224844545567,
    0.09972378565249672, 0.07384727982904729, -0.13547360506233205, 0.040268019240819755,
)


def gelu_and_slope(values):
    size = jnp.abs(values)
    base = 1.0 + (0.4 * 0.7071067811865476) * size
    t = pl.reciprocal(base, approx=True)
    t = t * (2.0 - base * t)
    tail = jnp.full_like(values, 0.5 * ERFC[-1])
    for factor in ERFC[-2::-1]:
        tail = tail * t + 0.5 * factor
    bell = jnp.exp2((-0.5 / math.log(2.0)) * values * values)
    tail = tail * t * bell
    share = jnp.where(values >= 0.0, 1.0 - tail, tail)
    return values * share, share + values * bell * 0.3989422804014327


def expert_forward_kernel(arrived_ref, weight_ref, act_ref, slope_ref, produced_ref, total_ref):
    c = pl.program_id(0)

    @pl.when(c == 0)
    def _():
        total_ref[...] = jnp.zeros_like(total_ref)

    preact = lax.dot_general(
        arrived_ref[...], weight_ref[:, :D], NT, preferred_element_type=F32
    )
    act, slope = gelu_and_slope(preact)
    act = act.astype(BF16)
    act_ref[...] = act
    slope_ref[...] = slope
    total_ref[...] += jnp.dot(act, weight_ref[:, D:], preferred_element_type=F32)

    @pl.when(c == pl.num_programs(0) - 1)
    def _():
        produced_ref[...] = total_ref[...].astype(BF16)


def expert_forward(arrived, weight):
    rows, hidden = arrived.shape[0], weight.shape[0]
    block = hidden // 12
    return pl.pallas_call(
        expert_forward_kernel,
        grid=(hidden // block,),
        out_shape=(
            jax.ShapeDtypeStruct((rows, hidden), BF16),
            jax.ShapeDtypeStruct((rows, hidden), F32),
            jax.ShapeDtypeStruct((rows, D), BF16),
        ),
        in_specs=[
            pl.BlockSpec((rows, D), lambda c: (0, 0)),
            pl.BlockSpec((block, 2 * D), lambda c: (c, 0)),
        ],
        out_specs=(
            pl.BlockSpec((rows, block), lambda c: (0, c)),
            pl.BlockSpec((rows, block), lambda c: (0, c)),
            pl.BlockSpec((rows, D), lambda c: (0, 0)),
        ),
        scratch_shapes=[pltpu.VMEM((rows, D), F32)],
        compiler_params=pltpu.CompilerParams(vmem_limit_bytes=VMEM_LIMIT),
        name="expert_forward",
    )(arrived, weight)


def expert_backward_kernel(incoming_ref, weight_ref, slope_ref, produced_ref, grad_ref, back_ref, total_ref):
    c = pl.program_id(0)

    @pl.when(c == 0)
    def _():
        total_ref[...] = jnp.zeros_like(total_ref)
        back_ref[:, :D] = produced_ref[...]

    grad_act = lax.dot_general(
        incoming_ref[...], weight_ref[:, D:], NT, preferred_element_type=F32
    )
    grad = (grad_act * slope_ref[...]).astype(BF16)
    grad_ref[...] = grad
    total_ref[...] += jnp.dot(grad, weight_ref[:, :D], preferred_element_type=F32)

    @pl.when(c == pl.num_programs(0) - 1)
    def _():
        back_ref[:, D:] = total_ref[...].astype(BF16)


def expert_backward(incoming, weight, slope, produced):
    rows, hidden = slope.shape
    block = hidden // 6
    whole = pl.BlockSpec((rows, D), lambda c: (0, 0))
    return pl.pallas_call(
        expert_backward_kernel,
        grid=(hidden // block,),
        out_shape=(
            jax.ShapeDtypeStruct((rows, hidden), BF16),
            jax.ShapeDtypeStruct((rows, 2 * D), BF16),
        ),
        in_specs=[
            whole,
            pl.BlockSpec((block, 2 * D), lambda c: (c, 0)),
            pl.BlockSpec((rows, block), lambda c: (0, c)),
            whole,
        ],
        out_specs=(
            pl.BlockSpec((rows, block), lambda c: (0, c)),
            pl.BlockSpec((rows, 2 * D), lambda c: (0, 0)),
        ),
        scratch_shapes=[pltpu.VMEM((rows, D), F32)],
        compiler_params=pltpu.CompilerParams(vmem_limit_bytes=VMEM_LIMIT),
        name="expert_backward",
    )(incoming, weight, slope, produced)


def weight_grad_kernel(hidden_ref, rows_ref, grad_ref):
    grad_ref[...] = lax.dot_general(
        hidden_ref[...], rows_ref[...], (((0,), (0,)), ((), ())), preferred_element_type=F32
    ).astype(BF16)


def weight_grad(hidden_rows, rows, name):
    count, hidden = hidden_rows.shape
    block = hidden // 4
    return pl.pallas_call(
        weight_grad_kernel,
        grid=(hidden // block,),
        in_specs=[
            pl.BlockSpec((count, block), lambda c: (0, c)),
            pl.BlockSpec((count, D), lambda c: (0, 0)),
        ],
        out_specs=pl.BlockSpec((block, D), lambda c: (c, 0)),
        out_shape=jax.ShapeDtypeStruct((hidden, D), BF16),
        compiler_params=pltpu.CompilerParams(vmem_limit_bytes=VMEM_LIMIT),
        name=name,
    )(hidden_rows, rows)


def input_grad_kernel(places_ref, rows_ref, weight_ref, middle_ref, normed_ref, factor_ref, gain_ref, out_ref):
    total = jnp.zeros((ROWS, D), F32)
    for c in range(N_SEQ):
        total += lax.dot_general(
            rows_ref[places_ref[c]], weight_ref[c], NT, preferred_element_type=F32
        )
    grad = total * gain_ref[...]
    out_ref[...] = middle_ref[...] + norm_back(grad, normed_ref[...], factor_ref[...])


def input_gradient(places, rows, weight, grad_middle, normed, factor, gain):
    return pl.pallas_call(
        input_grad_kernel,
        out_shape=jax.ShapeDtypeStruct((ROWS, D), F32),
        in_specs=[pl.BlockSpec(memory_space=pltpu.SMEM)] + in_vmem(6),
        out_specs=pl.BlockSpec(memory_space=pltpu.VMEM),
        compiler_params=pltpu.CompilerParams(vmem_limit_bytes=VMEM_LIMIT),
        name="input_gradient",
    )(places, rows, weight, grad_middle, normed, factor, gain)


def pass_y(value):
    return lax.ppermute(value, SEQ[0], [(0, 1), (1, 0)])


def gather_x(block, other, ready):
    both = jnp.concatenate([block, other])
    both = both if ready is None else after(both, ready)
    return lax.all_gather(both, SEQ[1], axis=0, tiled=True)


def scatter_x(value):
    return lax.psum_scatter(value, SEQ[1], scatter_dimension=0, tiled=True)


def sum_y(part):
    half = part.shape[0] // 2
    other = pass_y(part[half:])
    return part[:half].astype(F32) + other.astype(F32), other


def gather_dp(block):
    return exchange(jnp.broadcast_to(block, (N_DP, *block.shape)), DP)


def in_order(gathered):
    width = gathered.shape[-1]
    gathered = gathered.reshape(N_DP, N_SEQ, SHARD, width)
    return gathered.transpose(1, 0, 2, 3).reshape(D, width)


def shards(
    inputs,
    routes,
    buckets,
    norm1_gain,
    qkv_weight,
    out_weight,
    rel_bias,
    norm2_gain,
    router_projection_weight,
    expert_in,
    expert_out,
    cotangent,
):
    seq_index = lax.axis_index(SEQ)
    capacity = 10 * ROWS // (4 * N_DP)
    routed_rows = N_DP * capacity

    flat_in = inputs.reshape(ROWS, D)
    normed_one, factor_one = normalize(flat_in)
    normed = normed_one.astype(BF16)
    normed_other = pass_y(normed)

    parts = qkv_weight.reshape(SHARD, 3, 4, 3, HEAD_DIM)
    parts = jnp.concatenate([parts[:, :, :, c] for c in (0, 1, 2, 1)], axis=-1)
    parts = parts.reshape(SHARD, 3, N_SEQ, PAIR).transpose(2, 0, 1, 3).reshape(N_SEQ, SHARD, GROUP)
    extra = jnp.stack([norm1_gain, jnp.pad(rel_bias, (0, SHARD - rel_bias.shape[0]))], axis=1)
    extra = jnp.pad(extra, ((0, 0), (0, 126)))
    parts = jnp.concatenate([parts, jnp.broadcast_to(extra, (N_SEQ, SHARD, 128))], axis=-1)
    second = [out_weight, router_projection_weight, norm2_gain[:, None]]
    parts = [parts] + [jnp.broadcast_to(p, (N_SEQ, SHARD, p.shape[-1])) for p in second]
    parts = jnp.concatenate(parts, axis=-1)
    parts = jnp.pad(parts, ((0, 0), (0, 0), (0, -parts.shape[-1] % 128)))
    parts = exchange(parts, SEQ).reshape(N_SEQ * SHARD, parts.shape[-1])
    normed_other = after(normed_other, parts)
    is_low = lax.axis_index(SEQ[0]) == 0
    normed = jnp.stack(
        [jnp.where(is_low, normed, normed_other), jnp.where(is_low, normed_other, normed)]
    )
    normed_all = lax.all_gather(normed, SEQ[1])
    first = gather_dp(parts[:, : GROUP + 128])
    second = gather_dp(after(parts[:, GROUP + 128 :], first))

    expert_rows = jnp.concatenate([expert_in[0].T, expert_out[0]], axis=1)
    expert_full = gather_x(expert_rows, pass_y(expert_rows), (first, normed_all))
    first = in_order(first)
    normed_all = after(normed_all, first).transpose(1, 0, 2, 3).reshape(LENGTH, D)
    pair_weight = first[:, :GROUP]
    gain_one = first[:, GROUP].astype(F32)
    bias_table = first[:, GROUP + 1].reshape(N_ALL, SHARD)[:, : rel_bias.shape[0]]
    bias_table = bias_table.reshape(HEADS, BUCKETS)

    route_pairs = routes.reshape(ROWS, 2).T
    expert_range = jnp.arange(N_DP, dtype=jnp.int32)
    onehot = (route_pairs[:, :, None] == expert_range[None, None, :]).astype(F32)
    named = onehot[0] + onehot[1]
    earlier = (
        jnp.arange(ROWS, dtype=jnp.int32)[:, None] > jnp.arange(ROWS, dtype=jnp.int32)[None, :]
    ).astype(BF16)
    before = jnp.dot(earlier, named.astype(BF16), preferred_element_type=F32)
    slot = jnp.sum(onehot * before[None], axis=-1).astype(jnp.int32)
    target = (route_pairs * capacity + slot).reshape(2 * ROWS)
    slots = jnp.arange(routed_rows, dtype=jnp.int32)
    take_map = (target[:, None] == slots[None, :]).astype(BF16)
    send_map = (slots[:, None] == target[None, :]).astype(BF16)
    token_send = send_map[:, :ROWS] + send_map[:, ROWS:]
    token_take = take_map[:ROWS] + take_map[ROWS:]

    h_one = (normed_all.astype(F32) * gain_one).astype(BF16)
    qkv = jnp.dot(h_one, pair_weight, preferred_element_type=F32).astype(BF16)
    reach = jnp.concatenate([jnp.full((ROWS,), -1, jnp.int32), buckets])
    reach_onehot = reach[None, :] == jnp.arange(BUCKETS, dtype=jnp.int32)[:, None]
    group = seq_index // 2
    parity = seq_index % 2
    own = jnp.stack([3 * group + 2 * parity, 3 * group + 1])
    own_onehot = jnp.arange(HEADS, dtype=jnp.int32)[None, :] == own[:, None]
    own_bias = jnp.sum(
        jnp.where(own_onehot[:, :, None], bias_table.astype(F32)[None], 0.0), axis=1
    )
    distance_bias = jnp.sum(
        jnp.where(reach_onehot[None], own_bias[:, :, None], 0.0), axis=1
    )
    distance_bias = jnp.where(reach[None, :] < 0, MASKED, distance_bias)
    distance_bias = jnp.pad(distance_bias, ((0, 6), (0, 0)))
    shared_blocks = jnp.where(
        parity == 0, jnp.array([0, 3, 4, 7], jnp.int32), jnp.array([1, 2, 5, 6], jnp.int32)
    )
    items = jnp.concatenate([jnp.arange(TILES, dtype=jnp.int32), shared_blocks])
    attended_pair, lse = attention_forward(items, distance_bias, qkv)
    pair_other = pass_y(pair_weight)
    attended_pair, pair_other, second = lax.optimization_barrier(
        (attended_pair, pair_other, second)
    )
    second = in_order(second)
    out_full = second[:, :D].reshape(4, 3, HEAD_DIM, D)
    out_pairs = jnp.concatenate([out_full[:, c] for c in (0, 1, 2, 1)], axis=1).reshape(
        N_SEQ * PAIR, D
    )
    router_full = second[:, D : D + N_DP]
    gain_two = second[:, D + N_DP].astype(F32)
    attended = exchange(attended_pair.reshape(N_SEQ, ROWS, PAIR), SEQ)
    attended = attended.transpose(1, 0, 2).reshape(ROWS, N_SEQ * PAIR)
    middle = flat_in + jnp.dot(attended, out_pairs, preferred_element_type=F32)

    normed_two, factor_two = normalize(middle)
    h_two = (normed_two * gain_two).astype(BF16)
    outgoing = jnp.dot(token_send, h_two, preferred_element_type=F32).astype(BF16)
    arrived = exchange(outgoing.reshape(N_DP, capacity, D), DP).reshape(routed_rows, D)

    logits = jnp.dot(h_two, router_full, preferred_element_type=F32)
    chosen = jnp.sum(logits[None] * onehot, axis=-1)
    gates = jax.nn.softmax(chosen, axis=0)
    grad_out = cotangent.reshape(ROWS, D)
    grad_assign = (gates[:, :, None] * grad_out[None]).astype(BF16).reshape(2 * ROWS, D)
    outgoing_grad = jnp.dot(send_map, grad_assign, preferred_element_type=F32).astype(BF16)
    incoming = exchange(outgoing_grad.reshape(N_DP, capacity, D), DP).reshape(routed_rows, D)

    activated, slope, produced = expert_forward(arrived, expert_full)
    produced = after(produced, incoming)
    weight_pairs = gather_x(pair_weight, pair_other, arrived).reshape(N_SEQ, D, GROUP)
    grad_preact, back = expert_backward(incoming, expert_full, slope, produced)
    back = exchange(back.reshape(N_DP, capacity, 2 * D), DP).reshape(routed_rows, 2 * D)
    out_part = scatter_x(weight_grad(activated, incoming, "grad_expert_out"))
    out_shard, out_other = sum_y(out_part)
    in_part = scatter_x(
        after(weight_grad(grad_preact, arrived, "grad_expert_in"), weight_pairs)
    )
    returned, grad_back = back[:, :D], back[:, D:]

    picked = jnp.dot(take_map, returned, preferred_element_type=F32).reshape(2, ROWS, D)
    layer_out = middle + jnp.sum(gates[:, :, None] * picked, axis=0)
    grad_gates = jnp.sum(grad_out[None] * picked, axis=-1)
    grad_chosen = gates * (grad_gates - jnp.sum(gates * grad_gates, axis=0, keepdims=True))
    grad_logits = jnp.sum(grad_chosen[:, :, None] * onehot, axis=0)

    grad_h_two = jnp.dot(token_take, grad_back, preferred_element_type=F32)
    grad_h_two = grad_h_two + lax.dot_general(
        grad_logits, router_full.astype(F32), NT, precision=lax.Precision.HIGHEST
    )
    grad_router = jnp.dot(h_two.astype(F32).T, grad_logits, precision=lax.Precision.HIGHEST)
    grad_gain_two = jnp.sum(grad_h_two * normed_two, axis=0)
    grad_middle = grad_out + norm_back(grad_h_two * gain_two, normed_two, factor_two)
    grad_branch = grad_middle.astype(BF16)
    grad_attended = lax.dot_general(grad_branch, out_pairs, NT, preferred_element_type=F32)
    grad_attended = grad_attended.astype(BF16).reshape(ROWS, N_SEQ, PAIR).transpose(1, 0, 2)
    grad_pair = exchange(grad_attended, SEQ).reshape(LENGTH, PAIR)

    grad_out_pairs = jnp.einsum("tc,te->ce", attended, grad_branch, preferred_element_type=F32)
    grad_out_pairs = grad_out_pairs.reshape(4, 4, HEAD_DIM, D)
    grad_out_weight = jnp.stack(
        [grad_out_pairs[:, 0], grad_out_pairs[:, 1] + grad_out_pairs[:, 3], grad_out_pairs[:, 2]],
        axis=1,
    ).reshape(D, D)
    small = jnp.concatenate([grad_router, grad_gain_two[:, None]], axis=1)
    second_grads = jnp.concatenate([grad_out_weight.astype(BF16), *two_parts(small)], axis=1)
    second_grads = jnp.pad(second_grads, ((0, 0), (0, 7 * 128 - second_grads.shape[1])))
    second_grads = exchange(second_grads.reshape(N_ALL, SHARD, 7 * 128), SEQ_DP)
    second_sum = jnp.sum(second_grads.astype(F32), axis=0)
    out_grad = second_sum[:, :D]
    small_sum = second_sum[:, D : D + 17] + second_sum[:, D + 17 : D + 34]
    router_grad = small_sum[:, :N_DP]
    norm2_grad = small_sum[:, N_DP]

    grad_qkv, grad_reach = attention_backward(items, distance_bias, qkv, grad_pair, lse)
    grad_qkv = after(grad_qkv, (second_grads, out_other))
    grad_qkv_rows = exchange(grad_qkv.reshape(N_SEQ, ROWS, GROUP), SEQ)
    before_first = grad_qkv_rows
    in_shard, in_other = sum_y(after(in_part, grad_qkv_rows))
    in_shard = in_shard.T
    sources = jnp.arange(N_SEQ, dtype=jnp.int32)
    places = (sources % 2 ^ seq_index // 4) * 4 + sources // 2
    input_grad = input_gradient(
        places, grad_qkv_rows, weight_pairs, grad_middle, normed_one, factor_one, gain_one[None]
    )

    grad_pair_weight = jnp.einsum("td,te->de", h_one, grad_qkv, preferred_element_type=F32)
    grad_own_bias = jnp.sum(
        jnp.where(reach_onehot[None], grad_reach[:2, None, :], 0.0), axis=-1
    )
    grad_table = jnp.sum(
        jnp.where(own_onehot[:, :, None], grad_own_bias[:, None, :], 0.0), axis=0
    ).reshape(N_ALL, -1)
    grad_extra = jnp.stack(two_parts(grad_table), axis=-1)
    grad_extra = jnp.pad(grad_extra, ((0, 0), (0, SHARD - grad_extra.shape[1]), (0, 126)))
    first_grads = jnp.concatenate(
        [grad_pair_weight.astype(BF16).reshape(N_ALL, SHARD, GROUP), grad_extra], axis=-1
    )
    first_grads = exchange(after(first_grads, before_first), SEQ_DP)
    first_grads = after(first_grads, in_other).astype(F32)
    pair_sum = jnp.sum(first_grads.reshape(N_SEQ, N_DP, SHARD, GROUP + 128), axis=1)
    bias_sum = jnp.sum(pair_sum[:, : rel_bias.shape[0], GROUP : GROUP + 2], axis=(0, 2))
    pair_sum = pair_sum[:, :, :GROUP].reshape(4, 2, SHARD, 3, 2, HEAD_DIM)
    qkv_grad = jnp.stack(
        [pair_sum[:, 0, :, :, 0], pair_sum[:, 0, :, :, 1] + pair_sum[:, 1, :, :, 1], pair_sum[:, 1, :, :, 0]],
        axis=3,
    )
    qkv_grad = qkv_grad.transpose(1, 2, 0, 3, 4).reshape(SHARD, 3 * D)
    norm1_grad = jnp.sum(qkv_weight.astype(F32) * qkv_grad, axis=1) / norm1_gain.astype(F32)
    return (
        layer_out[None],
        input_grad[None],
        norm1_grad,
        qkv_grad,
        out_grad,
        bias_sum,
        norm2_grad,
        router_grad,
        in_shard[None],
        out_shard[None],
    )


def solution(mesh):
    torus = Mesh(mesh.devices.reshape(2, 4, 4, 2, 2), SEQ_DP)
    rows = P(DP, SEQ, None)
    spread = P(SEQ_DP)
    wide = P(SEQ_DP, None)
    in_specs = (
        rows,
        rows,
        P(),
        spread,
        wide,
        wide,
        spread,
        spread,
        wide,
        P(DP, None, SEQ),
        P(DP, SEQ, None),
        rows,
    )
    out_specs = (
        rows,
        rows,
        spread,
        wide,
        wide,
        spread,
        spread,
        wide,
        P(DP, None, SEQ),
        P(DP, SEQ, None),
    )
    return jax.shard_map(
        shards, mesh=torus, in_specs=in_specs, out_specs=out_specs, check_vma=False
    )
```
